32 devices in a mesh: variant: 4 (over y, x), vocab: 8 (over z, core).
Axes of the slice: x: 2, y: 2, z: 4, core: 2. Of those that a mesh axis runs over, the one named last changes fastest.
Arguments:
- teacher_hidden: bfloat16 [4, 256, 4096], P(None, None, ('variant', 'vocab')), may hold values from -24 to 24
- teacher_weight: bfloat16 [4096, 64128], P(None, ('vocab', 'variant')), may hold values from -1 to 1
- variant_ids: int32 [4], replicated, may hold values from 0 to 13
- temps: float32 [14], replicated, may hold values from 0.7 to 1.5
- student_hidden: bfloat16 [256, 2048], P(None, 'variant'), may hold values from -24 to 24
- student_weight: bfloat16 [2048, 64128], P('variant', 'vocab'), may hold values from -1 to 1
- token_ids: int32 [256], P('variant'), may hold values from 0 to 64127
- loss_mask: int32 [256], P('variant'), may hold values 0 or 1
Outputs:
- token_loss: float32 [256], P('variant')
- student_grad: float32 [2048, 64128], P('variant', 'vocab')
The draws below stay inside these ranges and needn't reach their ends.
All inputs are finite; a program needn't handle non-finite values. No bound on the sum of `loss_mask` on one device may be relied on, other than what follows from the above.
Results may differ from the reference program's by a relative error of at most 0.0025.
Values may be sent and summed in bfloat16 or wider, within the bound.
A program may use at most 192 MiB of HBM per device.

```python
import math
import jax
import jax.numpy as jnp
import numpy as np
from jax import lax

DT = 4096
DS = 2048
VOCAB = 64128
POLICIES = 14
TOK = 256
VARIANTS = 4


def hidden_draw(key, shape, salt):
    base = jax.random.normal(jax.random.fold_in(key, salt), shape, jnp.float32) * 3.0
    return jnp.clip(base, -24.0, 24.0)


def weight_draw(key, width, salt):
    base = jnp.clip(jax.random.normal(jax.random.fold_in(key, salt + 3), (width, VOCAB), jnp.float32), -6.0, 6.0) * width ** (-0.5)
    return base


def draw_teacher_hidden(key, part):
    return hidden_draw(key, (VARIANTS, TOK, DT), 100).astype(jnp.bfloat16)


def draw_teacher_weight(key, part):
    return weight_draw(key, DT, 100).astype(jnp.bfloat16)


def draw_student_hidden(key, part):
    return hidden_draw(key, (TOK, DS), 200).astype(jnp.bfloat16)


def draw_student_weight(key, part):
    return weight_draw(key, DS, 200).astype(jnp.bfloat16)


def with_ends(values, rng, low, top_value):
    shape = values.shape
    index_at = [jax.random.randint(jax.random.fold_in(rng, axis), (), 0, shape[axis]) for axis in range(len(shape))]
    values = values.at[tuple(index_at)].set(low)
    longest = shape.index(max(shape))
    index_at[longest] = (index_at[longest] + 1) % shape[longest]
    return values.at[tuple(index_at)].set(top_value)


def cumulative_ranks(count, lean):
    portions = [(1 << 20) // math.isqrt(grade ** lean) + 1 for grade in range(1, count + 1)]
    scale = 1 + sum(portions) // (1 << 30)
    return np.cumsum(np.array([max(1, weight // scale) for weight in portions]))


def ranked(stream_key, extent, amount, lean):
    grid = cumulative_ranks(amount, lean)
    pick = jax.random.randint(jax.random.fold_in(stream_key, 1), extent, 0, int(grid[amount - 1]))
    rank = jnp.searchsorted(jnp.asarray(grid, jnp.int32), pick, side="right")
    return jax.random.permutation(jax.random.fold_in(stream_key, 2), amount)[rank].astype(jnp.int32)


def setup_inputs(seed: int = 0) -> dict:
    streams_of = jax.random.split(jax.random.key(seed), 9)
    teacher_hidden = draw_teacher_hidden(jax.random.fold_in(streams_of[8], 71), 0)
    teacher_weight = draw_teacher_weight(jax.random.fold_in(streams_of[8], 71), 0)
    variant_ids = with_ends(jax.random.randint(streams_of[2], (VARIANTS,), 0, POLICIES), jax.random.fold_in(streams_of[2], 1), 0, POLICIES - 1).astype(jnp.int32)
    temps = jnp.clip(jnp.exp(jax.random.uniform(streams_of[3], (POLICIES,), jnp.float32, math.log(0.7), math.log(1.5))), 0.7, 1.5)
    student_hidden = draw_student_hidden(jax.random.fold_in(streams_of[8], 71), 0)
    student_weight = draw_student_weight(jax.random.fold_in(streams_of[8], 71), 0)
    token_ids = with_ends(ranked(streams_of[6], (TOK,), VOCAB, 2), jax.random.fold_in(streams_of[6], 3), 0, VOCAB - 1).astype(jnp.int32)
    loss_mask = with_ends((jax.random.randint(streams_of[7], (TOK,), 0, 4) < 3).astype(jnp.int32), jax.random.fold_in(streams_of[7], 1), 0, 1)
    return dict(teacher_hidden=teacher_hidden, teacher_weight=teacher_weight, variant_ids=variant_ids, temps=temps, student_hidden=student_hidden, student_weight=student_weight, token_ids=token_ids, loss_mask=loss_mask)


mix_weight = 0.5
loss_scale = 4096.0


def reference(teacher_hidden, teacher_weight, variant_ids, temps, student_hidden, student_weight, token_ids, loss_mask):
    chosen = temps[variant_ids]

    def add_variant(carry, inputs):
        hidden, tau = inputs
        scaled = jnp.dot(hidden, teacher_weight, preferred_element_type=jnp.float32) / tau
        top = jnp.max(scaled, axis=1, keepdims=True)
        expd = jnp.exp(scaled - top)
        return carry + expd / jnp.sum(expd, axis=1, keepdims=True), None

    start = jnp.zeros((teacher_hidden.shape[1], teacher_weight.shape[1]), jnp.float32)
    summed, _ = lax.scan(add_variant, start, (teacher_hidden, chosen))
    averaged = summed / VARIANTS
    logits = jnp.dot(student_hidden, student_weight, preferred_element_type=jnp.float32)
    top = jnp.max(logits, axis=1, keepdims=True)
    total = jnp.sum(jnp.exp(logits - top), axis=1, keepdims=True)
    log_probs = logits - (top + jnp.log(total))
    probs = jnp.exp(log_probs)
    onehot = token_ids[:, None] == jnp.arange(VOCAB, dtype=jnp.int32)[None, :]
    soft = jnp.sum(averaged * log_probs, axis=1)
    hard = jnp.sum(jnp.where(onehot, log_probs, 0.0), axis=1)
    maskf = loss_mask.astype(jnp.float32)
    token_loss = maskf * (-mix_weight * soft - (1.0 - mix_weight) * hard)
    error = (loss_scale * maskf[:, None] * (probs - mix_weight * averaged - (1.0 - mix_weight) * onehot.astype(jnp.float32))).astype(jnp.bfloat16)
    student_grad = jnp.dot(student_hidden.T, error, preferred_element_type=jnp.float32)
    return token_loss, student_grad
```

```python
import functools

import jax
import jax.numpy as jnp
from jax import lax
from jax.experimental import pallas as pl
from jax.experimental.pallas import tpu as pltpu
from jax.sharding import PartitionSpec as P

mix_weight = 0.5
loss_scale = 4096.0
MESH = pl.DeviceIdType.MESH


def gather_kernel(h_ref, ids_ref, out_ref, ids_out, send, recv, isend, irecv, local):
    v, w = lax.axis_index("variant"), lax.axis_index("vocab")
    z, c = w // 2, w % 2
    xn = v + 1 - 2 * (v % 2)
    yn = (v + 2) % 4
    dg = (xn + 2) % 4
    sib = w + 1 - 2 * c
    width = h_ref.shape[2]
    half = h_ref.shape[0] // 2

    partners = [(v, ((z + k) % 4) * 2 + c) for k in (1, 2, 3)] + [(xn, w), (yn, w), (dg, w), (v, sib)]
    barrier = pltpu.get_barrier_semaphore()
    for device in partners:
        pl.semaphore_signal(barrier, inc=1, device_id=device, device_id_type=MESH)
    pl.semaphore_wait(barrier, len(partners))

    def block(variant, k, lo=0, n=2 * half):
        column = (variant * 8 + ((z + 4 - k) % 4) * 2 + c) * width
        return out_ref.at[pl.ds(lo, n), :, pl.ds(pl.multiple_of(column, width), width)]

    started = []

    def push(src, dst, device, sem):
        copy = pltpu.make_async_remote_copy(
            src_ref=src, dst_ref=dst, send_sem=send.at[sem], recv_sem=recv.at[sem],
            device_id=device, device_id_type=MESH,
        )
        copy.start()
        started.append(copy)
        return copy

    own = pltpu.make_async_copy(h_ref, block(v, 0), local.at[0])
    own.start()
    own_ids = pltpu.make_async_copy(ids_ref, ids_out.at[v], local.at[1])
    own_ids.start()
    along = {k: push(h_ref, block(v, 0), (v, ((z + k) % 4) * 2 + c), k - 1) for k in (1, 2, 3)}
    id_copies = []
    for i, device in enumerate((xn, yn, dg)):
        copy = pltpu.make_async_remote_copy(
            src_ref=ids_ref, dst_ref=ids_out.at[v], send_sem=isend.at[i], recv_sem=irecv.at[i],
            device_id=(device, w), device_id_type=MESH,
        )
        copy.start()
        id_copies.append(copy)

    over_x, over_y, via_x, via_y, across = {}, {}, {}, {}, []

    def spread(k):
        src = h_ref if k == 0 else block(v, k)
        if k:
            along[k].wait_recv()
        over_x[k] = push(src, block(v, k), (xn, w), 3 + k)
        over_y[k] = push(src, block(v, k), (yn, w), 7 + k)
        across.append(push(src, block(v, k), (v, sib), 19 + k))

    def forward(k):
        over_x[k].wait_recv()
        via_x[k] = push(block(xn, k, 0, half), block(xn, k, 0, half), (yn, w), 11 + k)
        across.append(push(block(xn, k), block(xn, k), (v, sib), 23 + k))
        over_y[k].wait_recv()
        via_y[k] = push(block(yn, k, half, half), block(yn, k, half, half), (xn, w), 15 + k)
        across.append(push(block(yn, k), block(yn, k), (v, sib), 27 + k))

    def last(k):
        via_x[k].wait_recv()
        via_y[k].wait_recv()
        across.append(push(block(dg, k), block(dg, k), (v, sib), 31 + k))

    for k in range(6):
        if k < 4:
            spread(k)
        if 1 <= k < 5:
            forward(k - 1)
        if k >= 2:
            last(k - 2)
    for copy in across:
        copy.wait_recv()
    for copy in started:
        copy.wait_send()
    for copy in id_copies:
        copy.wait()
    own.wait()
    own_ids.wait()


def gather_inputs(hidden, ids, n_devices):
    v, t, d = hidden.shape
    return pl.pallas_call(
        gather_kernel,
        out_shape=(
            jax.ShapeDtypeStruct((v, t, d * n_devices), hidden.dtype),
            jax.ShapeDtypeStruct((4,) + ids.shape, ids.dtype),
        ),
        in_specs=[pl.BlockSpec(memory_space=pl.ANY)] * 2,
        out_specs=[pl.BlockSpec(memory_space=pl.ANY)] * 2,
        scratch_shapes=[
            pltpu.SemaphoreType.DMA((35,)),
            pltpu.SemaphoreType.DMA((35,)),
            pltpu.SemaphoreType.DMA((3,)),
            pltpu.SemaphoreType.DMA((3,)),
            pltpu.SemaphoreType.DMA((2,)),
        ],
        compiler_params=pltpu.CompilerParams(collective_id=0, has_side_effects=True),
    )(hidden, ids)


def merge(parts):
    top = functools.reduce(jnp.maximum, [p[0] for p in parts])
    scales = [jnp.exp(p[0] - top) for p in parts]
    total = sum(p[1] * s for p, s in zip(parts, scales))
    weighted = sum(p[2] * s for p, s in zip(parts, scales))
    return top, total, weighted


def stats_kernel(n1, n2, x_ref, out_ref, got1, mid, got2, s1, r1, s2, r2):
    v, w = lax.axis_index("variant"), lax.axis_index("vocab")
    firsts = [((v + k) % n1, w) for k in range(1, n1)]
    seconds = [(v, (w + k) % n2) for k in range(1, n2)]
    barrier = pltpu.get_barrier_semaphore()
    for device in firsts + seconds:
        pl.semaphore_signal(barrier, inc=1, device_id=device, device_id_type=MESH)
    pl.semaphore_wait(barrier, len(firsts) + len(seconds))

    def exchange(src, got, send, recv, devices):
        copies = []
        for k, device in enumerate(devices):
            copy = pltpu.make_async_remote_copy(
                src_ref=src, dst_ref=got.at[k], send_sem=send.at[k], recv_sem=recv.at[k],
                device_id=device, device_id_type=MESH,
            )
            copy.start()
            copies.append(copy)
        for copy in copies:
            copy.wait()
        return merge([[src[j] for j in range(3)]] + [[got[k, j] for j in range(3)] for k in range(len(devices))])

    for j, value in enumerate(exchange(x_ref, got1, s1, r1, firsts)):
        mid[j] = value
    for j, value in enumerate(exchange(mid, got2, s2, r2, seconds)):
        out_ref[j] = value


def merge_everywhere(stats, n1, n2):
    return pl.pallas_call(
        functools.partial(stats_kernel, n1, n2),
        out_shape=jax.ShapeDtypeStruct(stats.shape, stats.dtype),
        in_specs=[pl.BlockSpec(memory_space=pltpu.VMEM)],
        out_specs=pl.BlockSpec(memory_space=pltpu.VMEM),
        scratch_shapes=[
            pltpu.VMEM((n1 - 1,) + stats.shape, stats.dtype),
            pltpu.VMEM(stats.shape, stats.dtype),
            pltpu.VMEM((n2 - 1,) + stats.shape, stats.dtype),
            pltpu.SemaphoreType.DMA((n1 - 1,)),
            pltpu.SemaphoreType.DMA((n1 - 1,)),
            pltpu.SemaphoreType.DMA((n2 - 1,)),
            pltpu.SemaphoreType.DMA((n2 - 1,)),
        ],
        compiler_params=pltpu.CompilerParams(collective_id=1, has_side_effects=True),
    )(stats)


def on_device(
    teacher_hidden,
    teacher_weight,
    variant_ids,
    temps,
    student_hidden,
    student_weight,
    token_ids,
    loss_mask,
):
    n1, n2 = lax.axis_size("variant"), lax.axis_size("vocab")
    n_variant = teacher_hidden.shape[0]
    columns = teacher_weight.shape[1]
    rows = token_ids.shape[0]
    tokens = rows * n1
    categories = jnp.arange(temps.shape[0], dtype=jnp.int32)
    taus = jnp.sum(
        jnp.where(variant_ids[:, None] == categories[None, :], temps[None, :], 0.0), axis=1
    )
    partial = jnp.dot(student_weight.T, student_hidden.T, preferred_element_type=jnp.float32)
    logits = lax.psum_scatter(
        partial.reshape(n1, columns, tokens), "variant", scatter_dimension=0, tiled=False
    )
    ids = jnp.pad(jnp.stack([token_ids, loss_mask]), ((0, 6), (0, 128 - rows)))
    if (n1, n2) == (4, 8) and teacher_hidden.shape[2] % 128 == 0:
        hidden_all, ids_all = gather_inputs(teacher_hidden, ids, n1 * n2)
    else:
        hidden_all = lax.all_gather(teacher_hidden, ("variant", "vocab"), axis=2, tiled=True)
        ids_all = lax.all_gather(ids, "variant", axis=0)
    token_all = ids_all[:, 0, :rows].reshape(tokens)
    mask_all = ids_all[:, 1, :rows].reshape(tokens).astype(jnp.float32)

    scaled = (
        jnp.einsum("dc,vtd->vct", teacher_weight, hidden_all, preferred_element_type=jnp.float32)
        / taus[:, None, None]
    )
    t_max = jnp.max(scaled, axis=1)
    t_exp = jnp.exp(scaled - t_max[:, None, :])
    t_sum = jnp.sum(t_exp, axis=1)
    t_dot = jnp.sum(t_exp * logits[None], axis=1)
    s_max = jnp.max(logits, axis=0)
    s_sum = jnp.sum(jnp.exp(logits - s_max[None, :]), axis=0)
    here = lax.axis_index("vocab") * (columns * n1) + lax.axis_index("variant") * columns
    onehot = (here + jnp.arange(columns, dtype=jnp.int32))[:, None] == token_all[None, :]
    s_hit = jnp.sum(jnp.where(onehot, logits, 0.0), axis=0)

    zero = jnp.zeros_like(s_max)
    pad = [zero] * (-(n_variant + 2) % 8)
    stats = jnp.stack(
        [
            jnp.stack([t_max[i] for i in range(n_variant)] + [s_max, zero] + pad),
            jnp.stack([t_sum[i] for i in range(n_variant)] + [s_sum, zero] + pad),
            jnp.stack([t_dot[i] for i in range(n_variant)] + [zero, s_hit] + pad),
        ]
    )
    top, total, weighted = merge_everywhere(stats, n1, n2)
    lse = top[n_variant] + jnp.log(total[n_variant])
    hit = weighted[n_variant + 1]
    soft = jnp.sum(weighted[:n_variant] / total[:n_variant], axis=0) / n_variant - lse
    hard = hit - lse
    loss = mask_all * (-mix_weight * soft - (1.0 - mix_weight) * hard)
    token_loss = lax.dynamic_slice(loss, (lax.axis_index("variant") * rows,), (rows,))

    averaged = (
        jnp.sum(
            jnp.exp(scaled - top[:n_variant, None, :]) / total[:n_variant, None, :], axis=0
        )
        / n_variant
    )
    q = jnp.exp(logits - lse[None, :])
    error = (
        loss_scale
        * mask_all[None, :]
        * (q - mix_weight * averaged - (1.0 - mix_weight) * onehot.astype(jnp.float32))
    ).astype(jnp.bfloat16)
    error_all = lax.all_gather(error, "variant", axis=0).reshape(n1 * columns, tokens)
    grad = jnp.dot(error_all, student_hidden, preferred_element_type=jnp.float32)
    return (token_loss, grad.T)


def solution(mesh):
    in_specs = (
        P(None, None, ("variant", "vocab")),
        P(None, ("vocab", "variant")),
        P(),
        P(),
        P(None, "variant"),
        P("variant", "vocab"),
        P("variant"),
        P("variant"),
    )
    out_specs = (P("variant"), P("variant", "vocab"))
    return jax.shard_map(
        on_device, mesh=mesh, in_specs=in_specs, out_specs=out_specs, check_vma=False
    )
```

```python
import functools

import jax
import jax.numpy as jnp
from jax import lax
from jax.experimental import pallas as pl
from jax.experimental.pallas import tpu as pltpu
from jax.sharding import PartitionSpec as P

mix_weight = 0.5
loss_scale = 4096.0
MESH = pl.DeviceIdType.MESH


def gather_kernel(h_ref, ids_ref, out_ref, ids_out, send, recv, isend, irecv, local):
    v, w = lax.axis_index("variant"), lax.axis_index("vocab")
    z, c = w // 2, w % 2
    xn = v + 1 - 2 * (v % 2)
    yn = (v + 2) % 4
    dg = (xn + 2) % 4
    sib = w + 1 - 2 * c
    width = h_ref.shape[2]
    half = h_ref.shape[0] // 2

    partners = [(v, ((z + k) % 4) * 2 + c) for k in (1, 2, 3)] + [(xn, w), (yn, w), (dg, w), (v, sib)]
    barrier = pltpu.get_barrier_semaphore()
    for device in partners:
        pl.semaphore_signal(barrier, inc=1, device_id=device, device_id_type=MESH)
    pl.semaphore_wait(barrier, len(partners))

    def block(variant, k, lo=0, n=2 * half):
        column = (variant * 8 + ((z + 4 - k) % 4) * 2 + c) * width
        return out_ref.at[pl.ds(lo, n), :, pl.ds(pl.multiple_of(column, width), width)]

    started = []

    def push(src, dst, device, sem):
        copy = pltpu.make_async_remote_copy(
            src_ref=src, dst_ref=dst, send_sem=send.at[sem], recv_sem=recv.at[sem],
            device_id=device, device_id_type=MESH,
        )
        copy.start()
        started.append(copy)
        return copy

    own = pltpu.make_async_copy(h_ref, block(v, 0), local.at[0])
    own.start()
    own_ids = pltpu.make_async_copy(ids_ref, ids_out.at[v], local.at[1])
    own_ids.start()
    along = {k: push(h_ref, block(v, 0), (v, ((z + k) % 4) * 2 + c), k - 1) for k in (1, 2, 3)}
    id_copies = []
    for i, device in enumerate((xn, yn, dg)):
        copy = pltpu.make_async_remote_copy(
            src_ref=ids_ref, dst_ref=ids_out.at[v], send_sem=isend.at[i], recv_sem=irecv.at[i],
            device_id=(device, w), device_id_type=MESH,
        )
        copy.start()
        id_copies.append(copy)

    over_x, over_y, via_x, via_y, across = {}, {}, {}, {}, []

    def spread(k):
        src = h_ref if k == 0 else block(v, k)
        if k:
            along[k].wait_recv()
        over_x[k] = push(src, block(v, k), (xn, w), 3 + k)
        over_y[k] = push(src, block(v, k), (yn, w), 7 + k)
        across.append(push(src, block(v, k), (v, sib), 19 + k))

    def forward(k):
        over_x[k].wait_recv()
        via_x[k] = push(block(xn, k, 0, half), block(xn, k, 0, half), (yn, w), 11 + k)
        across.append(push(block(xn, k), block(xn, k), (v, sib), 23 + k))
        over_y[k].wait_recv()
        via_y[k] = push(block(yn, k, half, half), block(yn, k, half, half), (xn, w), 15 + k)
        across.append(push(block(yn, k), block(yn, k), (v, sib), 27 + k))

    def last(k):
        via_x[k].wait_recv()
        via_y[k].wait_recv()
        across.append(push(block(dg, k), block(dg, k), (v, sib), 31 + k))

    for k in range(6):
        if k < 4:
            spread(k)
        if 1 <= k < 5:
            forward(k - 1)
        if k >= 2:
            last(k - 2)
    for copy in across:
        copy.wait_recv()
    for copy in started:
        copy.wait_send()
    for copy in id_copies:
        copy.wait()
    own.wait()
    own_ids.wait()


def gather_inputs(hidden, ids, n_devices):
    v, t, d = hidden.shape
    return pl.pallas_call(
        gather_kernel,
        out_shape=(
            jax.ShapeDtypeStruct((v, t, d * n_devices), hidden.dtype),
            jax.ShapeDtypeStruct((4,) + ids.shape, ids.dtype),
        ),
        in_specs=[pl.BlockSpec(memory_space=pl.ANY)] * 2,
        out_specs=[pl.BlockSpec(memory_space=pl.ANY)] * 2,
        scratch_shapes=[
            pltpu.SemaphoreType.DMA((35,)),
            pltpu.SemaphoreType.DMA((35,)),
            pltpu.SemaphoreType.DMA((3,)),
            pltpu.SemaphoreType.DMA((3,)),
            pltpu.SemaphoreType.DMA((2,)),
        ],
        compiler_params=pltpu.CompilerParams(collective_id=0, has_side_effects=True),
    )(hidden, ids)


def merge(parts):
    top = functools.reduce(jnp.maximum, [p[0] for p in parts])
    scales = [jnp.exp(p[0] - top) for p in parts]
    total = sum(p[1] * s for p, s in zip(parts, scales))
    weighted = sum(p[2] * s for p, s in zip(parts, scales))
    return top, total, weighted


def stats_kernel(n1, n2, x_ref, out_ref, got1, mid, got2, s1, r1, s2, r2):
    v, w = lax.axis_index("variant"), lax.axis_index("vocab")
    firsts = [((v + k) % n1, w) for k in range(1, n1)]
    seconds = [(v, (w + k) % n2) for k in range(1, n2)]
    barrier = pltpu.get_barrier_semaphore()
    for device in firsts + seconds:
        pl.semaphore_signal(barrier, inc=1, device_id=device, device_id_type=MESH)
    pl.semaphore_wait(barrier, len(firsts) + len(seconds))

    def exchange(src, got, send, recv, devices):
        copies = []
        for k, device in enumerate(devices):
            copy = pltpu.make_async_remote_copy(
                src_ref=src, dst_ref=got.at[k], send_sem=send.at[k], recv_sem=recv.at[k],
                device_id=device, device_id_type=MESH,
            )
            copy.start()
            copies.append(copy)
        for copy in copies:
            copy.wait()
        return merge([[src[j] for j in range(3)]] + [[got[k, j] for j in range(3)] for k in range(len(devices))])

    for j, value in enumerate(exchange(x_ref, got1, s1, r1, firsts)):
        mid[j] = value
    for j, value in enumerate(exchange(mid, got2, s2, r2, seconds)):
        out_ref[j] = value


def merge_everywhere(stats, n1, n2):
    return pl.pallas_call(
        functools.partial(stats_kernel, n1, n2),
        out_shape=jax.ShapeDtypeStruct(stats.shape, stats.dtype),
        in_specs=[pl.BlockSpec(memory_space=pltpu.VMEM)],
        out_specs=pl.BlockSpec(memory_space=pltpu.VMEM),
        scratch_shapes=[
            pltpu.VMEM((n1 - 1,) + stats.shape, stats.dtype),
            pltpu.VMEM(stats.shape, stats.dtype),
            pltpu.VMEM((n2 - 1,) + stats.shape, stats.dtype),
            pltpu.SemaphoreType.DMA((n1 - 1,)),
            pltpu.SemaphoreType.DMA((n1 - 1,)),
            pltpu.SemaphoreType.DMA((n2 - 1,)),
            pltpu.SemaphoreType.DMA((n2 - 1,)),
        ],
        compiler_params=pltpu.CompilerParams(collective_id=1, has_side_effects=True),
    )(stats)


def error_kernel(e_ref, out_ref, send, recv, local):
    v, w = lax.axis_index("variant"), lax.axis_index("vocab")
    xn = v + 1 - 2 * (v % 2)
    yn = (v + 2) % 4
    barrier = pltpu.get_barrier_semaphore()
    for device in (xn, yn):
        pl.semaphore_signal(barrier, inc=1, device_id=(device, w), device_id_type=MESH)
    pl.semaphore_wait(barrier, 2)

    half = e_ref.shape[1] // 2

    def part(variant, i):
        return out_ref.at[variant, :, pl.ds(i * half, half)]

    def push(src, dst, device, sem):
        copy = pltpu.make_async_remote_copy(
            src_ref=src, dst_ref=dst, send_sem=send.at[sem], recv_sem=recv.at[sem],
            device_id=(device, w), device_id_type=MESH,
        )
        copy.start()
        return copy

    mine = [e_ref.at[:, pl.ds(i * half, half)] for i in range(2)]
    x0 = push(mine[0], part(v, 0), xn, 0)
    y1 = push(mine[1], part(v, 1), yn, 1)
    x1 = push(mine[1], part(v, 1), xn, 2)
    y0 = push(mine[0], part(v, 0), yn, 3)
    own = pltpu.make_async_copy(e_ref, out_ref.at[v], local.at[0])
    own.start()
    x0.wait_recv()
    via_x = push(part(xn, 0), part(xn, 0), yn, 4)
    y1.wait_recv()
    via_y = push(part(yn, 1), part(yn, 1), xn, 5)
    x1.wait_recv()
    y0.wait_recv()
    via_x.wait_recv()
    via_y.wait_recv()
    for copy in (x0, y1, x1, y0, via_x, via_y):
        copy.wait_send()
    own.wait()


def gather_errors(error):
    return pl.pallas_call(
        error_kernel,
        out_shape=jax.ShapeDtypeStruct((4,) + error.shape, error.dtype),
        in_specs=[pl.BlockSpec(memory_space=pl.ANY)],
        out_specs=pl.BlockSpec(memory_space=pl.ANY),
        scratch_shapes=[
            pltpu.SemaphoreType.DMA((6,)),
            pltpu.SemaphoreType.DMA((6,)),
            pltpu.SemaphoreType.DMA((1,)),
        ],
        compiler_params=pltpu.CompilerParams(collective_id=2, has_side_effects=True),
    )(error)


def on_device(
    teacher_hidden,
    teacher_weight,
    variant_ids,
    temps,
    student_hidden,
    student_weight,
    token_ids,
    loss_mask,
):
    n1, n2 = lax.axis_size("variant"), lax.axis_size("vocab")
    n_variant = teacher_hidden.shape[0]
    columns = teacher_weight.shape[1]
    rows = token_ids.shape[0]
    tokens = rows * n1
    categories = jnp.arange(temps.shape[0], dtype=jnp.int32)
    taus = jnp.sum(
        jnp.where(variant_ids[:, None] == categories[None, :], temps[None, :], 0.0), axis=1
    )
    partial = jnp.dot(student_weight.T, student_hidden.T, preferred_element_type=jnp.float32)
    logits = lax.psum_scatter(
        partial.reshape(n1, columns, tokens), "variant", scatter_dimension=0, tiled=False
    )
    ids = jnp.pad(jnp.stack([token_ids, loss_mask]), ((0, 6), (0, 128 - rows)))
    if (n1, n2) == (4, 8) and teacher_hidden.shape[2] % 128 == 0:
        hidden_all, ids_all = gather_inputs(teacher_hidden, ids, n1 * n2)
    else:
        hidden_all = lax.all_gather(teacher_hidden, ("variant", "vocab"), axis=2, tiled=True)
        ids_all = lax.all_gather(ids, "variant", axis=0)
    token_all = ids_all[:, 0, :rows].reshape(tokens)
    mask_all = ids_all[:, 1, :rows].reshape(tokens).astype(jnp.float32)

    scaled = (
        jnp.einsum("dc,vtd->vct", teacher_weight, hidden_all, preferred_element_type=jnp.float32)
        / taus[:, None, None]
    )
    t_max = jnp.max(scaled, axis=1)
    t_exp = jnp.exp(scaled - t_max[:, None, :])
    t_sum = jnp.sum(t_exp, axis=1)
    t_dot = jnp.sum(t_exp * logits[None], axis=1)
    s_max = jnp.max(logits, axis=0)
    s_sum = jnp.sum(jnp.exp(logits - s_max[None, :]), axis=0)
    here = lax.axis_index("vocab") * (columns * n1) + lax.axis_index("variant") * columns
    onehot = (here + jnp.arange(columns, dtype=jnp.int32))[:, None] == token_all[None, :]
    s_hit = jnp.sum(jnp.where(onehot, logits, 0.0), axis=0)

    zero = jnp.zeros_like(s_max)
    pad = [zero] * (-(n_variant + 2) % 8)
    stats = jnp.stack(
        [
            jnp.stack([t_max[i] for i in range(n_variant)] + [s_max, zero] + pad),
            jnp.stack([t_sum[i] for i in range(n_variant)] + [s_sum, zero] + pad),
            jnp.stack([t_dot[i] for i in range(n_variant)] + [zero, s_hit] + pad),
        ]
    )
    top, total, weighted = merge_everywhere(stats, n1, n2)
    lse = top[n_variant] + jnp.log(total[n_variant])
    hit = weighted[n_variant + 1]
    soft = jnp.sum(weighted[:n_variant] / total[:n_variant], axis=0) / n_variant - lse
    hard = hit - lse
    loss = mask_all * (-mix_weight * soft - (1.0 - mix_weight) * hard)
    token_loss = lax.dynamic_slice(loss, (lax.axis_index("variant") * rows,), (rows,))

    averaged = (
        jnp.sum(
            jnp.exp(scaled - top[:n_variant, None, :]) / total[:n_variant, None, :], axis=0
        )
        / n_variant
    )
    q = jnp.exp(logits - lse[None, :])
    error = (
        loss_scale
        * mask_all[None, :]
        * (q - mix_weight * averaged - (1.0 - mix_weight) * onehot.astype(jnp.float32))
    ).astype(jnp.bfloat16)
    if (n1, n2) == (4, 8) and tokens % 256 == 0:
        error_all = gather_errors(error)
    else:
        error_all = lax.all_gather(error, "variant", axis=0)
    error_all = error_all.reshape(n1 * columns, tokens)
    grad = jnp.dot(error_all, student_hidden, preferred_element_type=jnp.float32)
    return (token_loss, grad.T)


def solution(mesh):
    in_specs = (
        P(None, None, ("variant", "vocab")),
        P(None, ("vocab", "variant")),
        P(),
        P(),
        P(None, "variant"),
        P("variant", "vocab"),
        P("variant"),
        P("variant"),
    )
    out_specs = (P("variant"), P("variant", "vocab"))
    return jax.shard_map(
        on_device, mesh=mesh, in_specs=in_specs, out_specs=out_specs, check_vma=False
    )
```
